512 devices in a mesh: layer: 16 (over x, y_hi, core), dp: 32 (over y_lo, z).
Axes of the slice: x: 4, y: 8 (y_hi: 2, y_lo: 4; y = y_hi * 4 + y_lo), z: 8, core: 2. Of those that a mesh axis runs over, the one named last changes fastest.
Arguments:
- acts: bfloat16 [16, 8192, 4096], P('layer', 'dp'), may hold values from -6 to 6
- factor_old: bfloat16 [16, 4096, 4096], P('layer', 'dp'), as said below
- basis_old: bfloat16 [16, 4096, 256], P('layer', 'dp'), may hold values from -0.09375 to 0.09375
- grads: bfloat16 [16, 4096, 2048], P(None, 'dp', 'layer'), may hold values from -12 to 12
Outputs:
- new_basis: bfloat16 [16, 4096, 256], P('layer', 'dp')
- eigenvalues: bfloat16 [16, 256], P('layer')
- preconditioned: bfloat16 [16, 4096, 2048], P(None, 'dp', 'layer')
- applied_rows: float32 [16, 4096, 256], P('layer', 'dp')
The draws below stay inside these ranges and needn't reach their ends.
Inputs may be any that keep to these rules, and one draw needn't show every extreme that they name: `factor_old`: each block is symmetric with a positive diagonal that outweighs the spectral norm of its off-diagonal part.
All inputs are finite; a program needn't handle non-finite values.
Results may differ from the reference program's by a relative error of at most 0.0035.
Values may be sent and summed in bfloat16 or wider, within the bound.
No kernel may reach another device: no remote copies, remote signals or barrier semaphores. Data moves between devices by JAX's collectives and lax.ppermute only.
A program may use at most 64 MiB of HBM per device.

```python
import math
import jax
import jax.numpy as jnp
from jax import lax

BW = 4096
RANK = 256
OUTW = 2048
BLOCKS = 16
TOKENS = 8192


def draw_factor_old(key, part):
    key = jax.random.fold_in(key, 11)
    first_key, second_key = jax.random.split(key)
    raw = jax.random.normal(first_key, (BLOCKS, BW, BW), jnp.float32)
    upper = math.log(10.0)
    symmetric = (raw + jnp.swapaxes(raw, 1, 2)) * (0.2 / math.sqrt(2.0 * BW))
    diagonal = jnp.exp(jax.random.uniform(second_key, (BLOCKS, BW), jnp.float32, 0.0, upper))
    identity = jnp.eye(BW, dtype=jnp.float32)
    return (symmetric * (1.0 - identity) + diagonal[:, :, None] * identity).astype(jnp.bfloat16)


def raised(drawn, own_key, source, target, shards_of, factor):
    owner, partner = [(jnp.arange(drawn.shape[position]) // (drawn.shape[position] // shards_of)).reshape([-1 if axis == position else 1 for axis in range(drawn.ndim)]) for position in (source, target)]
    chosen = jax.random.permutation(own_key, shards_of)[partner]
    strong = (owner == chosen) | (owner == (partner + shards_of // 2) % shards_of)
    return jnp.where(strong, factor * drawn, drawn)


def levels(own_key, shape, shards, low, top_value):
    loudness, own = 1.0, jax.random.fold_in(own_key, 6)
    for position, shards_of in shards:
        heights = jnp.exp(jax.random.uniform(jax.random.fold_in(own, position), (shards_of,), jnp.float32, low / len(shards), top_value / len(shards)))
        loudness = loudness * jnp.repeat(heights, shape[position] // shards_of).reshape([-1 if axis == position else 1 for axis in range(len(shape))])
    return loudness


def noise(rng, shape, width, bound, shards=(), held_as=jnp.bfloat16):
    drawn = jax.random.normal(rng, shape, jnp.float32) * width
    if len(shards) > 0:
        drawn = levels(rng, shape, shards, -0.22, 0.18) * drawn
    return jnp.clip(drawn, min=-bound, max=bound).astype(held_as)


def gaussian_with(key, dims, spread, bound, cuts, heavy, kind=jnp.bfloat16):
    values = spread * jax.random.normal(key, dims, jnp.float32)
    if cuts:
        values = values * levels(key, dims, cuts, -0.22, 0.18)
    return jnp.clip(raised(values, jax.random.fold_in(key, 3), *heavy), -bound, bound).astype(kind)


def setup_inputs(seed: int = 0) -> dict:
    key_list = jax.random.split(jax.random.key(seed), 5)
    acts = gaussian_with(key_list[0], (BLOCKS, TOKENS, BW), 1.0, 6.0, ((0, 16), (1, 32)), (1, 2, 32, 2.75))
    factor_old = draw_factor_old(jax.random.fold_in(key_list[4], 71), 0)
    basis_old = noise(key_list[2], (BLOCKS, BW, RANK), BW ** -0.5, 0.09375, ((0, 16), (1, 32)))
    grads = gaussian_with(key_list[3], (BLOCKS, BW, OUTW), 2.0, 12.0, ((1, 32), (2, 16)), (1, 2, 32, 2.75))
    return dict(acts=acts, factor_old=factor_old, basis_old=basis_old, grads=grads)


def one_block(inputs):
    acts_b, factor_b, basis_b, grad_b = inputs
    projected = jnp.dot(acts_b.astype(jnp.float32), basis_b.astype(jnp.float32), preferred_element_type=jnp.float32).astype(jnp.bfloat16)
    token_sum = lax.dot_general(acts_b.astype(jnp.float32), projected.astype(jnp.float32), (((0,), (0,)), ((), ())), preferred_element_type=jnp.float32)
    applied = 0.25 * jnp.dot(factor_b.astype(jnp.float32), basis_b.astype(jnp.float32), preferred_element_type=jnp.float32) + 0.75 / TOKENS * token_sum
    applied_rows = applied * math.sqrt(BW)
    gram = jnp.dot(applied.T, applied, precision=lax.Precision.HIGHEST)
    lower = jnp.linalg.cholesky(gram)
    eigen_vals = jnp.diagonal(lower).astype(jnp.bfloat16)
    solved = lax.linalg.triangular_solve(lower, applied, left_side=False, lower=True, transpose_a=True)
    fresh = solved.astype(jnp.bfloat16)
    coupling = lax.dot_general(fresh.astype(jnp.float32), grad_b.astype(jnp.float32), (((0,), (0,)), ((), ())), preferred_element_type=jnp.float32)
    factors = 1.0 / (eigen_vals.astype(jnp.float32) + 2.0) - 0.5
    scaled = (factors[:, None] * coupling).astype(jnp.bfloat16)
    result = grad_b.astype(jnp.float32) * 0.5 + jnp.dot(fresh.astype(jnp.float32), scaled.astype(jnp.float32), preferred_element_type=jnp.float32)
    return (fresh, eigen_vals, result.astype(jnp.bfloat16), applied_rows)

def reference(acts, factor_old, basis_old, grads):
    fresh, eigen_vals, result, applied_rows = lax.map(one_block, (acts, factor_old, basis_old, grads))
    return (fresh, eigen_vals, result, applied_rows)
```

```python
import math

import jax
import jax.numpy as jnp
from jax import lax
from jax.sharding import PartitionSpec as P

decay_rate = 0.25
damping = 2.0
HIGHEST = lax.Precision.HIGHEST


def exchange(parts, axis):
    return lax.all_to_all(parts, axis, split_axis=0, concat_axis=0, tiled=True)


def gather(part, axis, copies):
    return exchange(jnp.broadcast_to(part[None], (copies,) + part.shape), axis)


def per_device(acts, factor_old, basis_old, grads):
    ranks = lax.axis_size("dp")
    token_rows, factor_rows = acts[0], factor_old[0]
    rank = basis_old.shape[2]
    width = factor_rows.shape[1]
    old_basis = gather(basis_old[0], "dp", ranks).reshape(width, rank)
    slab = exchange(grads, "layer")
    projected = jnp.dot(token_rows, old_basis, preferred_element_type=jnp.float32).astype(
        jnp.bfloat16
    )
    partial_sums = lax.dot_general(
        token_rows, projected, (((0,), (0,)), ((), ())), preferred_element_type=jnp.float32
    ).astype(jnp.bfloat16)
    parts = exchange(partial_sums.reshape(ranks, width // ranks, rank), "dp")
    summed = jnp.sum(parts.astype(jnp.float32), axis=0)
    total_tokens = token_rows.shape[0] * ranks
    applied = (
        decay_rate * jnp.dot(factor_rows, old_basis, preferred_element_type=jnp.float32)
        + (1.0 - decay_rate) / total_tokens * summed
    )
    applied_rows = applied * math.sqrt(width)
    gram_local = jnp.dot(applied.T, applied, precision=HIGHEST)
    gram_parts = exchange(gram_local.reshape(ranks, rank // ranks, rank), "dp")
    gram_rows = jnp.sum(gram_parts, axis=0)
    gram_total = gather(gram_rows, "dp", ranks).reshape(rank, rank)

    high = applied.astype(jnp.bfloat16)
    low = (applied - high.astype(jnp.float32)).astype(jnp.bfloat16)
    dims = (((1,), (0,)), ((), ()))
    cross = lax.dot_general(slab, high, dims, preferred_element_type=jnp.float32)
    cross = cross + lax.dot_general(slab, low, dims, preferred_element_type=jnp.float32)
    columns = slab.shape[0] * slab.shape[2]
    cross_parts = exchange(cross.reshape(ranks, columns // ranks, rank), "dp")
    cross_sum = jnp.sum(cross_parts, axis=0)

    lower = jnp.linalg.cholesky(gram_total)
    inverse = lax.linalg.triangular_solve(
        lower, jnp.eye(rank, dtype=jnp.float32), left_side=True, lower=True
    )
    eigen_vals = jnp.diagonal(lower).astype(jnp.bfloat16)
    fresh = lax.dot_general(
        applied, inverse, (((1,), (1,)), ((), ())), precision=HIGHEST
    ).astype(jnp.bfloat16)
    coupling = lax.dot_general(cross_sum, inverse, (((1,), (1,)), ((), ())), precision=HIGHEST)
    factors = 1.0 / (eigen_vals.astype(jnp.float32) + damping) - 1.0 / damping
    scaled_part = (coupling * factors[None, :]).astype(jnp.bfloat16)
    scaled = gather(scaled_part, "dp", ranks).reshape(slab.shape[0], slab.shape[2], rank)
    moved = lax.dot_general(
        fresh, scaled, (((1,), (2,)), ((), ())), preferred_element_type=jnp.float32
    )
    result = slab.astype(jnp.float32) / damping + jnp.swapaxes(moved, 0, 1)
    conditioned = exchange(result.astype(jnp.bfloat16), "layer")
    return (fresh[None], eigen_vals[None], conditioned, applied_rows[None])


def solution(mesh):
    in_specs = (
        P("layer", "dp", None),
        P("layer", "dp", None),
        P("layer", "dp", None),
        P(None, "dp", "layer"),
    )
    out_specs = (
        P("layer", "dp", None),
        P("layer", None),
        P(None, "dp", "layer"),
        P("layer", "dp", None),
    )
    return jax.shard_map(
        per_device, mesh=mesh, in_specs=in_specs, out_specs=out_specs, check_vma=False
    )
```

```python
import math

import jax
import jax.numpy as jnp
from jax import lax
from jax.experimental import pallas as pl
from jax.experimental.pallas import tpu as pltpu
from jax.sharding import Mesh, PartitionSpec as P

decay_rate = 0.25
damping = 2.0
f4 = jnp.float32
bf = jnp.bfloat16
PANEL = 32

LAYER = ("x", "yhi", "core")
DP = ("ylo", "z")
YS, ZS = 4, 8

TN = (((0,), (0,)), ((), ()))
NN = (((1,), (0,)), ((), ()))
NT = (((1,), (1,)), ((), ()))


def exchange(parts, axis):
    return lax.all_to_all(parts, axis, split_axis=0, concat_axis=0, tiled=True)


def gather(part, axis, copies):
    return exchange(jnp.broadcast_to(part[None], (copies,) + part.shape), axis)


def call(body, outs, flops, name):
    return pl.pallas_call(
        body,
        out_shape=outs,
        name=name,
        cost_estimate=pl.CostEstimate(flops=flops, bytes_accessed=1 << 20, transcendentals=0),
        compiler_params=pltpu.CompilerParams(vmem_limit_bytes=40 << 20),
    )


def dot(a, b, dims):
    return lax.dot_general(a, b, dims, preferred_element_type=f4)


def split(v):
    hi = v.astype(bf)
    rest = v - hi.astype(f4)
    mid = rest.astype(bf)
    return hi, mid, (rest - mid.astype(f4)).astype(bf)


def exact_dot(a, b, dims):
    (ca,), (cb,) = dims[0]
    h, m, l = split(a)
    left = jnp.concatenate([h, h, m, m, h, l], axis=ca)
    h, m, l = split(b)
    right = jnp.concatenate([h, m, h, m, l, h], axis=cb)
    return dot(left, right, dims)


def project_kernel(acts_ref, factor_ref, basis_ref, parts_ref, moved_ref):
    zs, ys, rows, rank = basis_ref.shape
    projected = jnp.zeros((acts_ref.shape[0], rank), f4)
    moved = jnp.zeros((factor_ref.shape[0], rank), f4)
    for y in range(ys):
        for z in range(0, zs, 2):
            at = (y * zs + z) * rows
            block = jnp.concatenate([basis_ref[z, y], basis_ref[z + 1, y]], axis=0)
            projected += dot(acts_ref[:, at : at + 2 * rows], block, NN)
            moved += dot(factor_ref[:, at : at + 2 * rows], block, NN)
    moved_ref[...] = moved
    turned = projected.T.astype(bf)
    for j in range(ys * zs):
        parts_ref[j] = dot(turned, acts_ref[:, j * rows : (j + 1) * rows], NN).astype(bf)


def applied_kernel(parts_ref, moved_ref, applied_ref, rows_ref, gram_ref, *, share, scale):
    total = parts_ref[0].astype(f4)
    for j in range(1, parts_ref.shape[0]):
        total = total + parts_ref[j].astype(f4)
    applied = decay_rate * moved_ref[...] + share * total.T
    applied_ref[...] = applied
    rows_ref[...] = applied * scale
    gram_ref[...] = exact_dot(applied, applied, TN)


def cross_kernel(applied_ref, slab_ref, cross_ref):
    hi, lo, _ = split(applied_ref[...])
    both = jnp.concatenate([hi, lo], axis=0)
    n = slab_ref.shape[2]
    for j in range(slab_ref.shape[0]):
        twice = jnp.concatenate([slab_ref[j], slab_ref[j]], axis=0)
        cross_ref[j * n : (j + 1) * n] = dot(twice, both, TN)


def reciprocal(x):
    r = pl.reciprocal(x, approx=True)
    r = r * (2.0 - x * r)
    return r * (2.0 - x * r)


def invert_factor(ref):
    n = ref.shape[0]
    halves = n // 128
    lane = lax.broadcasted_iota(jnp.int32, (8, 128), 1)
    row = lax.broadcasted_iota(jnp.int32, (8, 128), 0)

    def read(r, count, q):
        return ref[r : r + count, q * 128 : (q + 1) * 128]

    def write(r, count, q, v):
        ref[r : r + count, q * 128 : (q + 1) * 128] = v

    def splat(v, i, j):
        return jnp.broadcast_to(v[j // 128][i : i + 1, j % 128 : j % 128 + 1], (8, 128))

    def lanes(v, j):
        return jnp.broadcast_to(v[j // 128][:, j % 128 : j % 128 + 1], (8, 128))

    def rows(v, i):
        return [jnp.broadcast_to(h[i : i + 1, :], (8, 128)) for h in v]

    steps = PANEL // 8
    for p0 in range(0, n, PANEL):
        slabs = [[read(p0 + 8 * s, 8, q) for q in range(halves)] for s in range(steps)]
        for s in range(steps):
            k0 = p0 + 8 * s
            v = slabs[s]
            d = [[splat(v, i, k0 + j) for j in range(i + 1)] for i in range(8)]
            low = [[None] * 8 for _ in range(8)]
            root = []
            for j in range(8):
                r = reciprocal(d[j][j])
                root.append(lax.rsqrt(d[j][j]))
                for i in range(j + 1, 8):
                    low[i][j] = d[i][j] * r
                for k in range(j + 1, 8):
                    for i in range(k, 8):
                        d[i][k] = d[i][k] - low[i][j] * d[k][j]
            w = [[None] * 8 for _ in range(8)]
            for j in range(8):
                for i in range(j + 1, 8):
                    t = low[i][j]
                    for m in range(j + 1, i):
                        t = t + low[i][m] * w[m][j]
                    w[i][j] = -t
            for i in range(8):
                for j in range(i):
                    w[i][j] = w[i][j] * root[i]
                w[i][i] = root[i]
            src = list(v)
            h = k0 // 128
            off = lane + (h * 128 - k0)
            inside = (off >= 0) & (off < 8)
            src[h] = jnp.where(inside, jnp.where(off == row, 1.0, 0.0), v[h])
            new = [jnp.zeros((8, 128), f4) for _ in range(halves)]
            for m in range(8):
                column = jnp.where(row >= m, w[m][m], 0.0)
                for i in range(m + 1, 8):
                    column = jnp.where(row >= i, w[i][m], column)
                source = rows(src, m)
                new = [new[q] + column * source[q] for q in range(halves)]
            slabs[s] = new
            for q in range(halves):
                write(k0, 8, q, new[q])
            spread = [rows(new, j) for j in range(8)] if s < steps - 1 else None
            for t in range(s + 1, steps):
                u = slabs[t]
                b = [lanes(u, k0 + m) for m in range(8)]
                cur = list(u)
                cur[h] = jnp.where(inside, 0.0, u[h])
                for j in range(8):
                    c = w[j][0] * b[0]
                    for m in range(1, j + 1):
                        c = c + w[j][m] * b[m]
                    cur = [cur[q] - c * spread[j][q] for q in range(halves)]
                slabs[t] = cur
        e0 = p0 + PANEL
        if e0 < n:
            top = jnp.concatenate([jnp.concatenate(v, axis=1) for v in slabs], axis=0)
            ahead = lax.broadcasted_iota(jnp.int32, (PANEL, n), 1) - p0
            below = lax.broadcasted_iota(jnp.int32, (PANEL, n), 0)
            kept = jnp.where((ahead > below) & (ahead < PANEL), 0.0, top)
            out = exact_dot(top, kept, TN)
            for q in range(halves):
                old = read(e0, n - e0, q)
                at = lax.broadcasted_iota(jnp.int32, (n - e0, 128), 1) + (q * 128 - p0)
                old = jnp.where((at >= 0) & (at < PANEL), 0.0, old)
                write(e0, n - e0, q, old - out[e0:, q * 128 : (q + 1) * 128])


def factor_kernel(gram_ref, applied_ref, inverse_ref, eigen_ref, fresh_ref):
    n = gram_ref.shape[0]
    inverse_ref[...] = gram_ref[...]
    invert_factor(inverse_ref)
    a = lax.broadcasted_iota(jnp.int32, (n, n), 0)
    b = lax.broadcasted_iota(jnp.int32, (n, n), 1)
    inverse = jnp.where(a >= b, inverse_ref[...], 0.0)
    inverse_ref[...] = inverse
    diagonal = jnp.sum(jnp.where(a == b, inverse, 0.0), axis=0, keepdims=True)
    eigen_ref[...] = (1.0 / diagonal).astype(bf)
    fresh_ref[...] = exact_dot(applied_ref[...], inverse, NT).astype(bf)


def scale_kernel(cross_ref, inverse_ref, eigen_ref, scaled_ref):
    total = cross_ref[0]
    for j in range(1, cross_ref.shape[0]):
        total = total + cross_ref[j]
    coupling = exact_dot(total, inverse_ref[...], NT)
    factors = 1.0 / (eigen_ref[...].astype(f4) + damping) - 1.0 / damping
    scaled = (coupling * factors).astype(bf)
    for j in range(scaled_ref.shape[0]):
        scaled_ref[j] = scaled


def result_kernel(fresh_ref, scaled_ref, slab_ref, out_ref):
    fresh = fresh_ref[...]
    for j in range(slab_ref.shape[0]):
        chunks = []
        for c in (2 * j, 2 * j + 1):
            chunks.append(scaled_ref[(c % YS) * ZS + c // YS])
        moved = dot(fresh, jnp.concatenate(chunks, axis=0), NT)
        out_ref[j] = (slab_ref[j].astype(f4) / damping + moved).astype(bf)


def per_device(acts, factor_old, basis_old, grads):
    token_rows, factor_rows = acts[0], factor_old[0]
    ranks = YS * ZS
    rows, rank = basis_old.shape[1:]
    width = factor_rows.shape[1]
    tokens = token_rows.shape[0] * ranks
    blocks, _, cols = grads.shape
    flops = 2 * width * rank * token_rows.shape[0]

    near = gather(basis_old[0], "ylo", YS)
    old_basis = lax.all_gather(near, "z", axis=0, tiled=False)
    slab = exchange(grads, LAYER)
    old_basis, slab = lax.optimization_barrier((old_basis, slab))
    parts, moved = call(
        project_kernel,
        (
            jax.ShapeDtypeStruct((ranks, rank, rows), bf),
            jax.ShapeDtypeStruct((rows, rank), f4),
        ),
        5 * flops // 2,
        "project",
    )(token_rows, factor_rows, old_basis)
    parts = exchange(parts, DP)

    def applied_body(*refs):
        applied_kernel(*refs, share=(1.0 - decay_rate) / tokens, scale=math.sqrt(width))

    applied, applied_rows, gram_local = call(
        applied_body,
        (
            jax.ShapeDtypeStruct((rows, rank), f4),
            jax.ShapeDtypeStruct((rows, rank), f4),
            jax.ShapeDtypeStruct((rank, rank), f4),
        ),
        flops // 4,
        "applied",
    )(parts, moved)
    gram_parts = exchange(gram_local.reshape(ranks, rank // ranks, rank), DP)
    gram = gather(jnp.sum(gram_parts, axis=0), DP, ranks).reshape(rank, rank)

    cross = call(
        cross_kernel,
        jax.ShapeDtypeStruct((blocks * cols, rank), f4),
        flops // 2,
        "cross",
    )(applied, slab)
    cross = lax.psum_scatter(cross, "z", scatter_dimension=0, tiled=True)
    inverse, eigen, fresh = call(
        factor_kernel,
        (
            jax.ShapeDtypeStruct((rank, rank), f4),
            jax.ShapeDtypeStruct((1, rank), bf),
            jax.ShapeDtypeStruct((rows, rank), bf),
        ),
        20 * flops,
        "factor",
    )(gram, applied)
    cross, inverse = lax.optimization_barrier((cross, inverse))
    cross = exchange(cross.reshape(YS, blocks * cols // ranks, rank), "ylo")
    scaled = call(
        scale_kernel,
        jax.ShapeDtypeStruct((ranks, blocks * cols // ranks, rank), bf),
        flops // 8,
        "scale",
    )(cross, inverse, eigen)
    scaled = exchange(scaled, DP)
    result = call(
        result_kernel,
        jax.ShapeDtypeStruct((blocks, rows, cols), bf),
        flops // 2,
        "result",
    )(fresh, scaled, slab)
    conditioned = exchange(result, LAYER)
    return (fresh[None], eigen, conditioned, applied_rows[None])


def solution(mesh):
    fine = Mesh(mesh.devices.reshape(4, 2, 2, YS, ZS), LAYER + DP)
    in_specs = (
        P(LAYER, DP, None),
        P(LAYER, DP, None),
        P(LAYER, DP, None),
        P(None, DP, LAYER),
    )
    out_specs = (
        P(LAYER, DP, None),
        P(LAYER, None),
        P(None, DP, LAYER),
        P(LAYER, DP, None),
    )
    return jax.shard_map(
        per_device, mesh=fine, in_specs=in_specs, out_specs=out_specs, check_vma=False
    )
```

```python
import math

import jax
import jax.numpy as jnp
from jax import lax
from jax.experimental import pallas as pl
from jax.experimental.pallas import tpu as pltpu
from jax.sharding import Mesh, PartitionSpec as P

decay_rate = 0.25
damping = 2.0
f4 = jnp.float32
bf = jnp.bfloat16
PANEL = 32

LAYER = ("x", "yhi", "core")
DP = ("ylo", "z")
YS, ZS = 4, 8

TN = (((0,), (0,)), ((), ()))
NN = (((1,), (0,)), ((), ()))
NT = (((1,), (1,)), ((), ()))


def exchange(parts, axis):
    return lax.all_to_all(parts, axis, split_axis=0, concat_axis=0, tiled=True)


def gather(part, axis, copies):
    return exchange(jnp.broadcast_to(part[None], (copies,) + part.shape), axis)


def call(body, outs, flops, name, **more):
    return pl.pallas_call(
        body,
        out_shape=outs,
        **more,
        name=name,
        cost_estimate=pl.CostEstimate(flops=flops, bytes_accessed=1 << 20, transcendentals=0),
        compiler_params=pltpu.CompilerParams(vmem_limit_bytes=24 << 20),
    )


def dot(a, b, dims):
    return lax.dot_general(a, b, dims, preferred_element_type=f4)


def split(v):
    hi = v.astype(bf)
    rest = v - hi.astype(f4)
    mid = rest.astype(bf)
    return hi, mid, (rest - mid.astype(f4)).astype(bf)


def exact_dot(a, b, dims):
    (ca,), (cb,) = dims[0]
    h, m, l = split(a)
    left = jnp.concatenate([h, h, m, m, h, l], axis=ca)
    h, m, l = split(b)
    right = jnp.concatenate([h, m, h, m, l, h], axis=cb)
    return dot(left, right, dims)


def project_kernel(acts_ref, basis_ref, parts_ref):
    zs, ys, rows, rank = basis_ref.shape
    turned = basis_product(acts_ref, basis_ref).T.astype(bf)
    for j in range(ys * zs):
        parts_ref[j] = dot(turned, acts_ref[:, j * rows : (j + 1) * rows], NN).astype(bf)


def basis_product(left_ref, basis_ref):
    zs, ys, rows, rank = basis_ref.shape
    total = jnp.zeros((left_ref.shape[0], rank), f4)
    for y in range(ys):
        for z in range(0, zs, 2):
            at = (y * zs + z) * rows
            block = jnp.concatenate([basis_ref[z, y], basis_ref[z + 1, y]], axis=0)
            total += dot(left_ref[:, at : at + 2 * rows], block, NN)
    return total


def applied_kernel(parts_ref, factor_ref, basis_ref, applied_ref, rows_ref, *, share, scale):
    total = parts_ref[0].astype(f4)
    for j in range(1, parts_ref.shape[0]):
        total = total + parts_ref[j].astype(f4)
    applied = decay_rate * basis_product(factor_ref, basis_ref) + share * total.T
    applied_ref[...] = jnp.broadcast_to(applied[None], applied_ref.shape)
    rows_ref[...] = applied * scale


def turn_kernel(grads_ref, turned_ref):
    blocks, quarter = grads_ref.shape[0], turned_ref.shape[1]
    share = grads_ref.shape[2] // quarter
    for b in range(blocks):
        turned = grads_ref[b].astype(f4).T.astype(bf)
        for q in range(share):
            turned_ref[b * share + q] = turned[q * quarter : (q + 1) * quarter]


def turn_back_kernel(turned_ref, out_ref):
    blocks, quarter = out_ref.shape[0], turned_ref.shape[1]
    share = out_ref.shape[2] // quarter
    for b in range(blocks):
        block = jnp.concatenate([turned_ref[b * share + q] for q in range(share)], axis=0)
        out_ref[b] = block.astype(f4).T.astype(bf)


def slab_of(slab_ref, y, ys):
    return jnp.concatenate([slab_ref[j] for j in range(y, slab_ref.shape[0], ys)], axis=0)


def cross_kernel(applied_ref, slab_ref, cross_ref):
    ys = applied_ref.shape[0]
    total = jnp.zeros(cross_ref.shape, f4)
    for y in range(ys):
        hi, lo, _ = split(applied_ref[y])
        slab = slab_of(slab_ref, y, ys)
        twice = jnp.concatenate([slab, slab], axis=1)
        total += dot(twice, jnp.concatenate([hi, lo], axis=0), NN)
    cross_ref[...] = total


def gram_kernel(applied_ref, gram_ref):
    applied = jnp.concatenate([applied_ref[j] for j in range(applied_ref.shape[0])], axis=0)
    gram_ref[...] = exact_dot(applied, applied, TN)


def sum_kernel(parts_ref, total_ref):
    total = parts_ref[0]
    for j in range(1, parts_ref.shape[0]):
        total = total + parts_ref[j]
    total_ref[...] = jnp.broadcast_to(total[None], total_ref.shape)


def reciprocal(x):
    r = pl.reciprocal(x, approx=True)
    r = r * (2.0 - x * r)
    return r * (2.0 - x * r)


def invert_factor(ref):
    n = ref.shape[0]
    halves = n // 128
    lane = lax.broadcasted_iota(jnp.int32, (8, 128), 1)
    row = lax.broadcasted_iota(jnp.int32, (8, 128), 0)

    def read(r, count, q):
        return ref[r : r + count, q * 128 : (q + 1) * 128]

    def write(r, count, q, v):
        ref[r : r + count, q * 128 : (q + 1) * 128] = v

    def splat(v, i, j):
        return jnp.broadcast_to(v[j // 128][i : i + 1, j % 128 : j % 128 + 1], (8, 128))

    def lanes(v, j):
        return jnp.broadcast_to(v[j // 128][:, j % 128 : j % 128 + 1], (8, 128))

    def rows(v, i):
        return [jnp.broadcast_to(h[i : i + 1, :], (8, 128)) for h in v]

    steps = PANEL // 8
    for p0 in range(0, n, PANEL):
        slabs = [[read(p0 + 8 * s, 8, q) for q in range(halves)] for s in range(steps)]
        for s in range(steps):
            k0 = p0 + 8 * s
            v = slabs[s]
            d = [[splat(v, i, k0 + j) for j in range(i + 1)] for i in range(8)]
            low = [[None] * 8 for _ in range(8)]
            root = []
            for j in range(8):
                r = reciprocal(d[j][j])
                root.append(lax.rsqrt(d[j][j]))
                for i in range(j + 1, 8):
                    low[i][j] = d[i][j] * r
                for k in range(j + 1, 8):
                    for i in range(k, 8):
                        d[i][k] = d[i][k] - low[i][j] * d[k][j]
            w = [[None] * 8 for _ in range(8)]
            for j in range(8):
                for i in range(j + 1, 8):
                    t = low[i][j]
                    for m in range(j + 1, i):
                        t = t + low[i][m] * w[m][j]
                    w[i][j] = -t
            for i in range(8):
                for j in range(i):
                    w[i][j] = w[i][j] * root[i]
                w[i][i] = root[i]
            src = list(v)
            h = k0 // 128
            off = lane + (h * 128 - k0)
            inside = (off >= 0) & (off < 8)
            src[h] = jnp.where(inside, jnp.where(off == row, 1.0, 0.0), v[h])
            new = [jnp.zeros((8, 128), f4) for _ in range(halves)]
            for m in range(8):
                column = jnp.where(row >= m, w[m][m], 0.0)
                for i in range(m + 1, 8):
                    column = jnp.where(row >= i, w[i][m], column)
                source = rows(src, m)
                new = [new[q] + column * source[q] for q in range(halves)]
            slabs[s] = new
            for q in range(halves):
                write(k0, 8, q, new[q])
            spread = [rows(new, j) for j in range(8)] if s < steps - 1 else None
            for t in range(s + 1, steps):
                u = slabs[t]
                b = [lanes(u, k0 + m) for m in range(8)]
                cur = list(u)
                cur[h] = jnp.where(inside, 0.0, u[h])
                for j in range(8):
                    c = w[j][0] * b[0]
                    for m in range(1, j + 1):
                        c = c + w[j][m] * b[m]
                    cur = [cur[q] - c * spread[j][q] for q in range(halves)]
                slabs[t] = cur
        e0 = p0 + PANEL
        if e0 < n:
            top = jnp.concatenate([jnp.concatenate(v, axis=1) for v in slabs], axis=0)
            ahead = lax.broadcasted_iota(jnp.int32, (PANEL, n), 1) - p0
            below = lax.broadcasted_iota(jnp.int32, (PANEL, n), 0)
            kept = jnp.where((ahead > below) & (ahead < PANEL), 0.0, top)
            out = exact_dot(top, kept, TN)
            for q in range(halves):
                old = read(e0, n - e0, q)
                at = lax.broadcasted_iota(jnp.int32, (n - e0, 128), 1) + (q * 128 - p0)
                old = jnp.where((at >= 0) & (at < PANEL), 0.0, old)
                write(e0, n - e0, q, old - out[e0:, q * 128 : (q + 1) * 128])


def factor_kernel(gram_ref, inverse_ref, eigen_ref, scale_ref):
    n = gram_ref.shape[0]
    inverse_ref[...] = gram_ref[...]
    invert_factor(inverse_ref)
    a = lax.broadcasted_iota(jnp.int32, (n, n), 0)
    b = lax.broadcasted_iota(jnp.int32, (n, n), 1)
    inverse = jnp.where(a >= b, inverse_ref[...], 0.0)
    inverse_ref[...] = inverse
    diagonal = jnp.sum(jnp.where(a == b, inverse, 0.0), axis=0, keepdims=True)
    eigen = (1.0 / diagonal).astype(bf)
    eigen_ref[...] = eigen
    scale_ref[...] = 1.0 / (eigen.astype(f4) + damping) - 1.0 / damping


def fresh_kernel(place_ref, applied_ref, inverse_ref, fresh_ref, own_ref):
    for y in range(applied_ref.shape[0]):
        fresh_ref[y] = exact_dot(applied_ref[y], inverse_ref[...], NT).astype(bf)
    own_ref[...] = fresh_ref[place_ref[0]]


def scale_kernel(cross_ref, inverse_ref, scale_ref, scaled_ref):
    coupling = exact_dot(cross_ref[...], inverse_ref[...], NT)
    scaled = (coupling * scale_ref[...]).astype(bf)
    for j in range(scaled_ref.shape[0]):
        scaled_ref[j] = scaled


def result_kernel(fresh_ref, scaled_ref, slab_ref, out_ref):
    ys, quarter = fresh_ref.shape[0], slab_ref.shape[1]
    scaled = jnp.concatenate([scaled_ref[j] for j in range(scaled_ref.shape[0])], axis=0)
    for y in range(ys):
        moved = dot(scaled, fresh_ref[y], NT)
        result = (slab_of(slab_ref, y, ys).astype(f4) / damping + moved).astype(bf)
        for j in range(out_ref.shape[0] // ys):
            out_ref[j * ys + y] = result[j * quarter : (j + 1) * quarter]


def per_device(acts, factor_old, basis_old, grads):
    token_rows, factor_rows = acts[0], factor_old[0]
    ranks = YS * ZS
    rows, rank = basis_old.shape[1:]
    width = factor_rows.shape[1]
    tokens = token_rows.shape[0] * ranks
    blocks, _, cols = grads.shape
    flops = 2 * width * rank * token_rows.shape[0]

    wide_columns = blocks * cols // YS
    chunk = wide_columns // ZS
    blocked = jax.ShapeDtypeStruct((blocks * YS, cols // YS, rows), bf)

    near = gather(basis_old[0], "ylo", YS)
    old_basis = lax.all_gather(near, "z", axis=0, tiled=False)
    slab = exchange(call(turn_kernel, blocked, flops // 64, "turn")(grads), LAYER + ("ylo",))
    old_basis, slab = lax.optimization_barrier((old_basis, slab))
    parts = call(
        project_kernel,
        jax.ShapeDtypeStruct((ranks, rank, rows), bf),
        2 * flops,
        "project",
    )(token_rows, old_basis)
    parts = exchange(parts, DP)

    def applied_body(*refs):
        applied_kernel(*refs, share=(1.0 - decay_rate) / tokens, scale=math.sqrt(width))

    applied, applied_rows = call(
        applied_body,
        (
            jax.ShapeDtypeStruct((YS, rows, rank), f4),
            jax.ShapeDtypeStruct((rows, rank), f4),
        ),
        flops // 2,
        "applied",
    )(parts, factor_rows, old_basis)
    applied = exchange(applied, "ylo")
    cross = call(
        cross_kernel, jax.ShapeDtypeStruct((wide_columns, rank), f4), flops // 2, "cross"
    )(applied, slab)
    cross, applied = lax.optimization_barrier((cross, applied))
    cross = lax.psum_scatter(cross, "z", scatter_dimension=0, tiled=True)
    gram = call(gram_kernel, jax.ShapeDtypeStruct((rank, rank), f4), flops, "gram")(applied)
    factor_out = (
        jax.ShapeDtypeStruct((rank, rank), f4),
        jax.ShapeDtypeStruct((1, rank), bf),
        jax.ShapeDtypeStruct((1, rank), f4),
    )

    def factored(gram):
        parts = exchange(gram.reshape(ZS, rank // ZS, rank), "z")
        total = call(
            sum_kernel, jax.ShapeDtypeStruct((ZS, rank // ZS, rank), f4), flops // 64, "sum"
        )(parts)
        total = exchange(total, "z").reshape(rank, rank)
        return call(factor_kernel, factor_out, 20 * flops, "factor")(total)

    inverse, eigen, scale = lax.cond(
        lax.axis_index("z") < ZS,
        factored,
        lambda _: tuple(jnp.zeros(v.shape, v.dtype) for v in factor_out),
        gram,
    )
    place = lax.axis_index("ylo").astype(jnp.int32).reshape(1)
    vmem, smem = pl.BlockSpec(memory_space=pltpu.VMEM), pl.BlockSpec(memory_space=pltpu.SMEM)
    wide_fresh, fresh = call(
        fresh_kernel,
        (
            jax.ShapeDtypeStruct((YS, rows, rank), bf),
            jax.ShapeDtypeStruct((rows, rank), bf),
        ),
        2 * flops,
        "fresh",
        in_specs=[smem, vmem, vmem],
    )(place, applied, inverse)
    scaled = call(
        scale_kernel,
        jax.ShapeDtypeStruct((ZS, chunk, rank), bf),
        flops // 8,
        "scale",
    )(cross, inverse, scale)
    scaled = exchange(scaled, "z")
    result = call(result_kernel, blocked, flops // 2, "result")(wide_fresh, scaled, slab)
    result = exchange(result, LAYER + ("ylo",))
    conditioned = call(
        turn_back_kernel,
        jax.ShapeDtypeStruct((blocks, rows, cols), bf),
        flops // 64,
        "turn_back",
    )(result)
    return (fresh[None], eigen, conditioned, applied_rows[None])


def solution(mesh):
    fine = Mesh(mesh.devices.reshape(4, 2, 2, YS, ZS), LAYER + DP)
    in_specs = (
        P(LAYER, DP, None),
        P(LAYER, DP, None),
        P(LAYER, DP, None),
        P(None, DP, LAYER),
    )
    out_specs = (
        P(LAYER, DP, None),
        P(LAYER, None),
        P(None, DP, LAYER),
        P(LAYER, DP, None),
    )
    return jax.shard_map(
        per_device, mesh=fine, in_specs=in_specs, out_specs=out_specs, check_vma=False
    )
```

```python
import math

import jax
import jax.numpy as jnp
from jax import lax
from jax.experimental import pallas as pl
from jax.experimental.pallas import tpu as pltpu
from jax.sharding import Mesh, PartitionSpec as P

decay_rate = 0.25
damping = 2.0
f4 = jnp.float32
bf = jnp.bfloat16
PANEL = 32

LAYER = ("x", "yhi", "core")
Y = ("ypair", "yside")
DP = Y + ("z",)
YS, ZS = 4, 8

TN = (((0,), (0,)), ((), ()))
NN = (((1,), (0,)), ((), ()))
NT = (((1,), (1,)), ((), ()))


def exchange(parts, axis):
    return lax.all_to_all(parts, axis, split_axis=0, concat_axis=0, tiled=True)


def gather(part, axis, copies):
    return exchange(jnp.broadcast_to(part[None], (copies,) + part.shape), axis)


def call(body, outs, flops, name, **more):
    return pl.pallas_call(
        body,
        out_shape=outs,
        **more,
        name=name,
        cost_estimate=pl.CostEstimate(flops=flops, bytes_accessed=1 << 20, transcendentals=0),
        compiler_params=pltpu.CompilerParams(vmem_limit_bytes=24 << 20),
    )


def dot(a, b, dims):
    return lax.dot_general(a, b, dims, preferred_element_type=f4)


def split(v):
    hi = v.astype(bf)
    rest = v - hi.astype(f4)
    mid = rest.astype(bf)
    return hi, mid, (rest - mid.astype(f4)).astype(bf)


def exact_dot(a, b, dims):
    (ca,), (cb,) = dims[0]
    h, m, l = split(a)
    left = jnp.concatenate([h, h, m, m, h, l], axis=ca)
    h, m, l = split(b)
    right = jnp.concatenate([h, m, h, m, l, h], axis=cb)
    return dot(left, right, dims)


def columns(ref, pair, side, quarter, first=0, count=None):
    at = (2 * pair + side) * quarter + first
    return ref[:, pl.ds(pl.multiple_of(at, 128), count or quarter)]


def deal_kernel(place_ref, acts_ref, out_ref):
    quarter = out_ref.shape[1] // 2
    for pair in range(2):
        out_ref[:, pair * quarter : (pair + 1) * quarter] = columns(
            acts_ref, pair, 1 - place_ref[0], quarter
        )


def project_kernel(acts_ref, basis_ref, turned_ref):
    turned_ref[...] = basis_product(acts_ref, basis_ref).T.astype(bf)


def token_kernel(place_ref, turned_ref, other_ref, acts_ref, got_ref, parts_ref):
    parts, _, rows = parts_ref.shape
    zs = parts // 2
    quarter = zs * rows
    for pair in range(2):
        for z in range(0, zs, 2):
            own = columns(acts_ref, pair, place_ref[0], quarter, z * rows, 2 * rows)
            at = pair * quarter + z * rows
            both = dot(turned_ref[...], own, NN)
            both += dot(other_ref[...], got_ref[:, at : at + 2 * rows], NN)
            parts_ref[pair * zs + z] = both[:, :rows].astype(bf)
            parts_ref[pair * zs + z + 1] = both[:, rows:].astype(bf)


def basis_product(left_ref, basis_ref):
    zs, ys, rows, rank = basis_ref.shape
    total = jnp.zeros((left_ref.shape[0], rank), f4)
    for y in range(ys):
        for z in range(0, zs, 2):
            at = (y * zs + z) * rows
            block = jnp.concatenate([basis_ref[z, y], basis_ref[z + 1, y]], axis=0)
            total += dot(left_ref[:, at : at + 2 * rows], block, NN)
    return total


def applied_kernel(parts_ref, factor_ref, basis_ref, applied_ref, rows_ref, *, share, scale):
    total = parts_ref[0].astype(f4)
    for j in range(1, parts_ref.shape[0]):
        total = total + parts_ref[j].astype(f4)
    applied = decay_rate * basis_product(factor_ref, basis_ref) + share * total.T
    applied_ref[...] = jnp.broadcast_to(applied[None], applied_ref.shape)
    rows_ref[...] = applied * scale


def turn_kernel(grads_ref, turned_ref):
    blocks, quarter = grads_ref.shape[0], turned_ref.shape[1]
    share = grads_ref.shape[2] // quarter
    for b in range(blocks):
        turned = grads_ref[b].astype(f4).T.astype(bf)
        for q in range(share):
            turned_ref[b * share + q] = turned[q * quarter : (q + 1) * quarter]


def turn_back_kernel(turned_ref, out_ref):
    blocks, quarter = out_ref.shape[0], turned_ref.shape[1]
    share = out_ref.shape[2] // quarter
    for b in range(blocks):
        block = jnp.concatenate([turned_ref[b * share + q] for q in range(share)], axis=0)
        out_ref[b] = block.astype(f4).T.astype(bf)


def slab_of(slab_ref, y, ys):
    return jnp.concatenate([slab_ref[j] for j in range(y, slab_ref.shape[0], ys)], axis=0)


def cross_kernel(applied_ref, slab_ref, cross_ref):
    ys, quarter = applied_ref.shape[0], slab_ref.shape[1]
    split_rows = [split(applied_ref[y]) for y in range(ys)]
    both = jnp.concatenate([v[0] for v in split_rows] + [v[1] for v in split_rows], axis=0)
    group = 4
    for j in range(0, slab_ref.shape[0] // ys, group):
        blocks = []
        for y in range(ys):
            held = [slab_ref[i * ys + y] for i in range(j, j + group)]
            blocks.append(jnp.concatenate(held, axis=0))
        left = jnp.concatenate(blocks + blocks, axis=1)
        cross_ref[j * quarter : (j + group) * quarter] = dot(left, both, NN)


def gram_kernel(applied_ref, gram_ref):
    applied = jnp.concatenate([applied_ref[j] for j in range(applied_ref.shape[0])], axis=0)
    gram_ref[...] = exact_dot(applied, applied, TN)


def sum_kernel(parts_ref, total_ref):
    total = parts_ref[0]
    for j in range(1, parts_ref.shape[0]):
        total = total + parts_ref[j]
    total_ref[...] = jnp.broadcast_to(total[None], total_ref.shape)


def reciprocal(x):
    r = pl.reciprocal(x, approx=True)
    r = r * (2.0 - x * r)
    return r * (2.0 - x * r)


def invert_factor(ref):
    n = ref.shape[0]
    halves = n // 128
    lane = lax.broadcasted_iota(jnp.int32, (8, 128), 1)
    row = lax.broadcasted_iota(jnp.int32, (8, 128), 0)

    def read(r, count, q):
        return ref[r : r + count, q * 128 : (q + 1) * 128]

    def write(r, count, q, v):
        ref[r : r + count, q * 128 : (q + 1) * 128] = v

    def splat(v, i, j):
        return jnp.broadcast_to(v[j // 128][i : i + 1, j % 128 : j % 128 + 1], (8, 128))

    def lanes(v, j):
        return jnp.broadcast_to(v[j // 128][:, j % 128 : j % 128 + 1], (8, 128))

    def rows(v, i):
        return [jnp.broadcast_to(h[i : i + 1, :], (8, 128)) for h in v]

    steps = PANEL // 8
    for p0 in range(0, n, PANEL):
        slabs = [[read(p0 + 8 * s, 8, q) for q in range(halves)] for s in range(steps)]
        for s in range(steps):
            k0 = p0 + 8 * s
            v = slabs[s]
            d = [[splat(v, i, k0 + j) for j in range(i + 1)] for i in range(8)]
            low = [[None] * 8 for _ in range(8)]
            root = []
            for j in range(8):
                r = reciprocal(d[j][j])
                root.append(lax.rsqrt(d[j][j]))
                for i in range(j + 1, 8):
                    low[i][j] = d[i][j] * r
                for k in range(j + 1, 8):
                    for i in range(k, 8):
                        d[i][k] = d[i][k] - low[i][j] * d[k][j]
            w = [[None] * 8 for _ in range(8)]
            for j in range(8):
                for i in range(j + 1, 8):
                    t = low[i][j]
                    for m in range(j + 1, i):
                        t = t + low[i][m] * w[m][j]
                    w[i][j] = -t
            for i in range(8):
                for j in range(i):
                    w[i][j] = w[i][j] * root[i]
                w[i][i] = root[i]
            src = list(v)
            h = k0 // 128
            off = lane + (h * 128 - k0)
            inside = (off >= 0) & (off < 8)
            src[h] = jnp.where(inside, jnp.where(off == row, 1.0, 0.0), v[h])
            new = [jnp.zeros((8, 128), f4) for _ in range(halves)]
            for m in range(8):
                column = jnp.where(row >= m, w[m][m], 0.0)
                for i in range(m + 1, 8):
                    column = jnp.where(row >= i, w[i][m], column)
                source = rows(src, m)
                new = [new[q] + column * source[q] for q in range(halves)]
            slabs[s] = new
            for q in range(halves):
                write(k0, 8, q, new[q])
            spread = [rows(new, j) for j in range(8)] if s < steps - 1 else None
            for t in range(s + 1, steps):
                u = slabs[t]
                b = [lanes(u, k0 + m) for m in range(8)]
                cur = list(u)
                cur[h] = jnp.where(inside, 0.0, u[h])
                for j in range(8):
                    c = w[j][0] * b[0]
                    for m in range(1, j + 1):
                        c = c + w[j][m] * b[m]
                    cur = [cur[q] - c * spread[j][q] for q in range(halves)]
                slabs[t] = cur
        e0 = p0 + PANEL
        if e0 < n:
            top = jnp.concatenate([jnp.concatenate(v, axis=1) for v in slabs], axis=0)
            ahead = lax.broadcasted_iota(jnp.int32, (PANEL, n), 1) - p0
            below = lax.broadcasted_iota(jnp.int32, (PANEL, n), 0)
            kept = jnp.where((ahead > below) & (ahead < PANEL), 0.0, top)
            out = exact_dot(top, kept, TN)
            for q in range(halves):
                old = read(e0, n - e0, q)
                at = lax.broadcasted_iota(jnp.int32, (n - e0, 128), 1) + (q * 128 - p0)
                old = jnp.where((at >= 0) & (at < PANEL), 0.0, old)
                write(e0, n - e0, q, old - out[e0:, q * 128 : (q + 1) * 128])


def factor_kernel(gram_ref, inverse_ref, eigen_ref, scale_ref):
    n = gram_ref.shape[0]
    inverse_ref[...] = gram_ref[...]
    invert_factor(inverse_ref)
    a = lax.broadcasted_iota(jnp.int32, (n, n), 0)
    b = lax.broadcasted_iota(jnp.int32, (n, n), 1)
    inverse = jnp.where(a >= b, inverse_ref[...], 0.0)
    inverse_ref[...] = inverse
    diagonal = jnp.sum(jnp.where(a == b, inverse, 0.0), axis=0, keepdims=True)
    eigen = (1.0 / diagonal).astype(bf)
    eigen_ref[...] = eigen
    scale_ref[...] = 1.0 / (eigen.astype(f4) + damping) - 1.0 / damping


def fresh_kernel(place_ref, applied_ref, inverse_ref, fresh_ref, own_ref):
    for y in range(applied_ref.shape[0]):
        fresh_ref[y] = exact_dot(applied_ref[y], inverse_ref[...], NT).astype(bf)
    own_ref[...] = fresh_ref[place_ref[0]]


def scale_kernel(cross_ref, inverse_ref, scale_ref, scaled_ref):
    coupling = exact_dot(cross_ref[...], inverse_ref[...], NT)
    scaled = (coupling * scale_ref[...]).astype(bf)
    for j in range(scaled_ref.shape[0]):
        scaled_ref[j] = scaled


def result_kernel(fresh_ref, scaled_ref, slab_ref, out_ref):
    ys, quarter = fresh_ref.shape[0], slab_ref.shape[1]
    scaled = jnp.concatenate([scaled_ref[j] for j in range(scaled_ref.shape[0])], axis=0)
    for y in range(ys):
        moved = dot(scaled, fresh_ref[y], NT)
        result = (slab_of(slab_ref, y, ys).astype(f4) / damping + moved).astype(bf)
        for j in range(out_ref.shape[0] // ys):
            out_ref[j * ys + y] = result[j * quarter : (j + 1) * quarter]


def per_device(acts, factor_old, basis_old, grads):
    token_rows, factor_rows = acts[0], factor_old[0]
    ranks = YS * ZS
    rows, rank = basis_old.shape[1:]
    width = factor_rows.shape[1]
    tokens = token_rows.shape[0] * ranks
    blocks, _, cols = grads.shape
    flops = 2 * width * rank * token_rows.shape[0]

    wide_columns = blocks * cols // YS
    chunk = wide_columns // ZS
    blocked = jax.ShapeDtypeStruct((blocks * YS, cols // YS, rows), bf)

    near = gather(basis_old[0], Y, YS)
    old_basis = lax.all_gather(near, "z", axis=0, tiled=False)
    place = lax.axis_index(Y).astype(jnp.int32).reshape(1)
    vmem, smem = pl.BlockSpec(memory_space=pltpu.VMEM), pl.BlockSpec(memory_space=pltpu.SMEM)
    side = lax.axis_index("yside").astype(jnp.int32).reshape(1)

    def swap(part):
        return lax.ppermute(part, "yside", [(0, 1), (1, 0)])

    tokens_here = token_rows.shape[0]
    got = swap(
        call(
            deal_kernel,
            jax.ShapeDtypeStruct((tokens_here, width // 2), bf),
            flops // 64,
            "deal",
            in_specs=[smem, vmem],
        )(side, token_rows)
    )
    slab = lax.cond(
        lax.axis_index("z") < ZS,
        lambda v: exchange(call(turn_kernel, blocked, flops // 64, "turn")(v), LAYER + Y),
        lambda _: jnp.zeros(blocked.shape, bf),
        grads,
    )
    old_basis, slab, got = lax.optimization_barrier((old_basis, slab, got))
    turned = call(
        project_kernel, jax.ShapeDtypeStruct((rank, tokens_here), bf), flops, "project"
    )(token_rows, old_basis)
    parts = call(
        token_kernel,
        jax.ShapeDtypeStruct((ranks // 2, rank, rows), bf),
        flops,
        "tokens",
        in_specs=[smem] + [vmem] * 4,
    )(side, turned, swap(turned), token_rows, got)
    parts = exchange(parts, ("ypair", "z"))

    def applied_body(*refs):
        applied_kernel(*refs, share=(1.0 - decay_rate) / tokens, scale=math.sqrt(width))

    applied, applied_rows = call(
        applied_body,
        (
            jax.ShapeDtypeStruct((YS, rows, rank), f4),
            jax.ShapeDtypeStruct((rows, rank), f4),
        ),
        flops // 2,
        "applied",
    )(parts, factor_rows, old_basis)
    applied = exchange(applied, Y)
    cross = call(
        cross_kernel, jax.ShapeDtypeStruct((wide_columns, rank), f4), flops // 2, "cross"
    )(applied, slab)
    cross, applied = lax.optimization_barrier((cross, applied))
    cross = lax.psum_scatter(cross, "z", scatter_dimension=0, tiled=True)
    gram = call(gram_kernel, jax.ShapeDtypeStruct((rank, rank), f4), flops, "gram")(applied)
    factor_out = (
        jax.ShapeDtypeStruct((rank, rank), f4),
        jax.ShapeDtypeStruct((1, rank), bf),
        jax.ShapeDtypeStruct((1, rank), f4),
    )

    def factored(gram):
        parts = exchange(gram.reshape(ZS, rank // ZS, rank), "z")
        total = call(
            sum_kernel, jax.ShapeDtypeStruct((ZS, rank // ZS, rank), f4), flops // 64, "sum"
        )(parts)
        total = exchange(total, "z").reshape(rank, rank)
        return call(factor_kernel, factor_out, 20 * flops, "factor")(total)

    inverse, eigen, scale = lax.cond(
        lax.axis_index("z") < ZS,
        factored,
        lambda _: tuple(jnp.zeros(v.shape, v.dtype) for v in factor_out),
        gram,
    )
    wide_fresh, fresh = call(
        fresh_kernel,
        (
            jax.ShapeDtypeStruct((YS, rows, rank), bf),
            jax.ShapeDtypeStruct((rows, rank), bf),
        ),
        2 * flops,
        "fresh",
        in_specs=[smem, vmem, vmem],
    )(place, applied, inverse)
    cross, wide_fresh = lax.optimization_barrier((cross, wide_fresh))
    scaled = call(
        scale_kernel,
        jax.ShapeDtypeStruct((ZS, chunk, rank), bf),
        flops // 8,
        "scale",
    )(cross, inverse, scale)
    scaled = exchange(scaled, "z")
    result = call(result_kernel, blocked, flops // 2, "result")(wide_fresh, scaled, slab)
    result = exchange(result, LAYER + Y)
    conditioned = call(
        turn_back_kernel,
        jax.ShapeDtypeStruct((blocks, rows, cols), bf),
        flops // 64,
        "turn_back",
    )(result)
    return (fresh[None], eigen, conditioned, applied_rows[None])


def solution(mesh):
    fine = Mesh(mesh.devices.reshape(4, 2, 2, YS // 2, 2, ZS), LAYER + DP)
    in_specs = (
        P(LAYER, DP, None),
        P(LAYER, DP, None),
        P(LAYER, DP, None),
        P(None, DP, LAYER),
    )
    out_specs = (
        P(LAYER, DP, None),
        P(LAYER, None),
        P(None, DP, LAYER),
        P(LAYER, DP, None),
    )
    return jax.shard_map(
        per_device, mesh=fine, in_specs=in_specs, out_specs=out_specs, check_vma=False
    )
```

```python
import math

import jax
import jax.numpy as jnp
from jax import lax
from jax.experimental import pallas as pl
from jax.experimental.pallas import tpu as pltpu
from jax.sharding import Mesh, PartitionSpec as P

decay_rate = 0.25
damping = 2.0
f4 = jnp.float32
bf = jnp.bfloat16
PANEL = 32

LAYER = ("x", "yhi", "core")
Y = ("ypair", "yside")
DP = Y + ("z",)
YS, ZS = 4, 8

TN = (((0,), (0,)), ((), ()))
NN = (((1,), (0,)), ((), ()))
NT = (((1,), (1,)), ((), ()))


def exchange(parts, axis):
    return lax.all_to_all(parts, axis, split_axis=0, concat_axis=0, tiled=True)


def gather(part, axis, copies):
    return exchange(jnp.broadcast_to(part[None], (copies,) + part.shape), axis)


def call(body, outs, flops, name, **more):
    return pl.pallas_call(
        body,
        out_shape=outs,
        **more,
        name=name,
        cost_estimate=pl.CostEstimate(flops=flops, bytes_accessed=1 << 20, transcendentals=0),
        compiler_params=pltpu.CompilerParams(vmem_limit_bytes=24 << 20),
    )


def dot(a, b, dims):
    return lax.dot_general(a, b, dims, preferred_element_type=f4)


def split(v):
    hi = v.astype(bf)
    rest = v - hi.astype(f4)
    mid = rest.astype(bf)
    return hi, mid, (rest - mid.astype(f4)).astype(bf)


def exact_dot(a, b, dims):
    (ca,), (cb,) = dims[0]
    h, m, l = split(a)
    left = jnp.concatenate([h, h, m, m, h, l], axis=ca)
    h, m, l = split(b)
    right = jnp.concatenate([h, m, h, m, l, h], axis=cb)
    return dot(left, right, dims)


def columns(ref, pair, side, quarter, first=0, count=None):
    at = (2 * pair + side) * quarter + first
    return ref[:, pl.ds(pl.multiple_of(at, 128), count or quarter)]


def deal_kernel(place_ref, acts_ref, out_ref):
    quarter = out_ref.shape[1] // 2
    for pair in range(2):
        out_ref[:, pair * quarter : (pair + 1) * quarter] = columns(
            acts_ref, pair, 1 - place_ref[0], quarter
        )


def project_kernel(acts_ref, basis_ref, turned_ref):
    turned_ref[...] = basis_product(acts_ref, basis_ref).T.astype(bf)


def token_kernel(place_ref, turned_ref, other_ref, acts_ref, got_ref, parts_ref):
    parts, _, rows = parts_ref.shape
    zs = parts // 2
    quarter = zs * rows
    for pair in range(2):
        for z in range(0, zs, 2):
            own = columns(acts_ref, pair, place_ref[0], quarter, z * rows, 2 * rows)
            at = pair * quarter + z * rows
            both = dot(turned_ref[...], own, NN)
            both += dot(other_ref[...], got_ref[:, at : at + 2 * rows], NN)
            parts_ref[pair * zs + z] = both[:, :rows].astype(bf)
            parts_ref[pair * zs + z + 1] = both[:, rows:].astype(bf)


def basis_product(left_ref, basis_ref):
    zs, ys, rows, rank = basis_ref.shape
    total = jnp.zeros((left_ref.shape[0], rank), f4)
    for y in range(ys):
        for z in range(0, zs, 2):
            at = (y * zs + z) * rows
            block = jnp.concatenate([basis_ref[z, y], basis_ref[z + 1, y]], axis=0)
            total += dot(left_ref[:, at : at + 2 * rows], block, NN)
    return total


def moved_kernel(factor_ref, basis_ref, moved_ref):
    moved_ref[...] = decay_rate * basis_product(factor_ref, basis_ref)


def applied_kernel(parts_ref, moved_ref, applied_ref, rows_ref, *, share, scale):
    total = parts_ref[0].astype(f4)
    for j in range(1, parts_ref.shape[0]):
        total = total + parts_ref[j].astype(f4)
    applied = moved_ref[...] + share * total.T
    applied_ref[...] = jnp.broadcast_to(applied[None], applied_ref.shape)
    rows_ref[...] = applied * scale


def turn_kernel(grads_ref, turned_ref):
    blocks, quarter = grads_ref.shape[0], turned_ref.shape[1]
    share = grads_ref.shape[2] // quarter
    for b in range(blocks):
        turned = grads_ref[b].astype(f4).T.astype(bf)
        for q in range(share):
            turned_ref[b * share + q] = turned[q * quarter : (q + 1) * quarter]


def turn_back_kernel(turned_ref, out_ref):
    blocks, quarter = out_ref.shape[0], turned_ref.shape[1]
    share = out_ref.shape[2] // quarter
    for b in range(blocks):
        block = jnp.concatenate([turned_ref[b * share + q] for q in range(share)], axis=0)
        out_ref[b] = block.astype(f4).T.astype(bf)


def slab_of(slab_ref, y, ys):
    return jnp.concatenate([slab_ref[j] for j in range(y, slab_ref.shape[0], ys)], axis=0)


def cross_kernel(applied_ref, slab_ref, cross_ref):
    ys, quarter = applied_ref.shape[0], slab_ref.shape[1]
    split_rows = [split(applied_ref[y]) for y in range(ys)]
    both = jnp.concatenate([v[0] for v in split_rows] + [v[1] for v in split_rows], axis=0)
    group = 4
    for j in range(0, slab_ref.shape[0] // ys, group):
        blocks = []
        for y in range(ys):
            held = [slab_ref[i * ys + y] for i in range(j, j + group)]
            blocks.append(jnp.concatenate(held, axis=0))
        left = jnp.concatenate(blocks + blocks, axis=1)
        cross_ref[j * quarter : (j + group) * quarter] = dot(left, both, NN)


def gram_kernel(applied_ref, gram_ref):
    applied = jnp.concatenate([applied_ref[j] for j in range(applied_ref.shape[0])], axis=0)
    gram_ref[...] = exact_dot(applied, applied, TN)


def sum_kernel(parts_ref, total_ref):
    total = parts_ref[0]
    for j in range(1, parts_ref.shape[0]):
        total = total + parts_ref[j]
    total_ref[...] = jnp.broadcast_to(total[None], total_ref.shape)


def reciprocal(x):
    r = pl.reciprocal(x, approx=True)
    r = r * (2.0 - x * r)
    return r * (2.0 - x * r)


def invert_factor(ref):
    n = ref.shape[0]
    halves = n // 128
    lane = lax.broadcasted_iota(jnp.int32, (8, 128), 1)
    row = lax.broadcasted_iota(jnp.int32, (8, 128), 0)

    def read(r, count, q):
        return ref[r : r + count, q * 128 : (q + 1) * 128]

    def write(r, count, q, v):
        ref[r : r + count, q * 128 : (q + 1) * 128] = v

    def splat(v, i, j):
        return jnp.broadcast_to(v[j // 128][i : i + 1, j % 128 : j % 128 + 1], (8, 128))

    def lanes(v, j):
        return jnp.broadcast_to(v[j // 128][:, j % 128 : j % 128 + 1], (8, 128))

    def rows(v, i):
        return [jnp.broadcast_to(h[i : i + 1, :], (8, 128)) for h in v]

    steps = PANEL // 8
    for p0 in range(0, n, PANEL):
        slabs = [[read(p0 + 8 * s, 8, q) for q in range(halves)] for s in range(steps)]
        for s in range(steps):
            k0 = p0 + 8 * s
            v = slabs[s]
            d = [[splat(v, i, k0 + j) for j in range(i + 1)] for i in range(8)]
            low = [[None] * 8 for _ in range(8)]
            root = []
            for j in range(8):
                r = reciprocal(d[j][j])
                root.append(lax.rsqrt(d[j][j]))
                for i in range(j + 1, 8):
                    low[i][j] = d[i][j] * r
                for k in range(j + 1, 8):
                    for i in range(k, 8):
                        d[i][k] = d[i][k] - low[i][j] * d[k][j]
            w = [[None] * 8 for _ in range(8)]
            for j in range(8):
                for i in range(j + 1, 8):
                    t = low[i][j]
                    for m in range(j + 1, i):
                        t = t + low[i][m] * w[m][j]
                    w[i][j] = -t
            for i in range(8):
                for j in range(i):
                    w[i][j] = w[i][j] * root[i]
                w[i][i] = root[i]
            src = list(v)
            h = k0 // 128
            off = lane + (h * 128 - k0)
            inside = (off >= 0) & (off < 8)
            src[h] = jnp.where(inside, jnp.where(off == row, 1.0, 0.0), v[h])
            new = [jnp.zeros((8, 128), f4) for _ in range(halves)]
            for m in range(8):
                column = jnp.where(row >= m, w[m][m], 0.0)
                for i in range(m + 1, 8):
                    column = jnp.where(row >= i, w[i][m], column)
                source = rows(src, m)
                new = [new[q] + column * source[q] for q in range(halves)]
            slabs[s] = new
            for q in range(halves):
                write(k0, 8, q, new[q])
            spread = [rows(new, j) for j in range(8)] if s < steps - 1 else None
            for t in range(s + 1, steps):
                u = slabs[t]
                b = [lanes(u, k0 + m) for m in range(8)]
                cur = list(u)
                cur[h] = jnp.where(inside, 0.0, u[h])
                for j in range(8):
                    c = w[j][0] * b[0]
                    for m in range(1, j + 1):
                        c = c + w[j][m] * b[m]
                    cur = [cur[q] - c * spread[j][q] for q in range(halves)]
                slabs[t] = cur
        e0 = p0 + PANEL
        if e0 < n:
            top = jnp.concatenate([jnp.concatenate(v, axis=1) for v in slabs], axis=0)
            ahead = lax.broadcasted_iota(jnp.int32, (PANEL, n), 1) - p0
            below = lax.broadcasted_iota(jnp.int32, (PANEL, n), 0)
            kept = jnp.where((ahead > below) & (ahead < PANEL), 0.0, top)
            out = exact_dot(top, kept, TN)
            for q in range(halves):
                old = read(e0, n - e0, q)
                at = lax.broadcasted_iota(jnp.int32, (n - e0, 128), 1) + (q * 128 - p0)
                old = jnp.where((at >= 0) & (at < PANEL), 0.0, old)
                write(e0, n - e0, q, old - out[e0:, q * 128 : (q + 1) * 128])


def factor_kernel(gram_ref, inverse_ref, eigen_ref, scale_ref):
    n = gram_ref.shape[0]
    inverse_ref[...] = gram_ref[...]
    invert_factor(inverse_ref)
    a = lax.broadcasted_iota(jnp.int32, (n, n), 0)
    b = lax.broadcasted_iota(jnp.int32, (n, n), 1)
    inverse = jnp.where(a >= b, inverse_ref[...], 0.0)
    inverse_ref[...] = inverse
    diagonal = jnp.sum(jnp.where(a == b, inverse, 0.0), axis=0, keepdims=True)
    eigen = (1.0 / diagonal).astype(bf)
    eigen_ref[...] = eigen
    scale_ref[...] = 1.0 / (eigen.astype(f4) + damping) - 1.0 / damping


def fresh_kernel(place_ref, applied_ref, inverse_ref, fresh_ref, own_ref):
    for y in range(applied_ref.shape[0]):
        fresh_ref[y] = exact_dot(applied_ref[y], inverse_ref[...], NT).astype(bf)
    own_ref[...] = fresh_ref[place_ref[0]]


def scale_kernel(cross_ref, inverse_ref, scale_ref, scaled_ref):
    coupling = exact_dot(cross_ref[...], inverse_ref[...], NT)
    scaled = (coupling * scale_ref[...]).astype(bf)
    for j in range(scaled_ref.shape[0]):
        scaled_ref[j] = scaled


def result_kernel(fresh_ref, scaled_ref, slab_ref, out_ref):
    ys, quarter = fresh_ref.shape[0], slab_ref.shape[1]
    scaled = jnp.concatenate([scaled_ref[j] for j in range(scaled_ref.shape[0])], axis=0)
    for y in range(ys):
        moved = dot(scaled, fresh_ref[y], NT)
        result = (slab_of(slab_ref, y, ys).astype(f4) / damping + moved).astype(bf)
        for j in range(out_ref.shape[0] // ys):
            out_ref[j * ys + y] = result[j * quarter : (j + 1) * quarter]


def per_device(acts, factor_old, basis_old, grads):
    token_rows, factor_rows = acts[0], factor_old[0]
    ranks = YS * ZS
    rows, rank = basis_old.shape[1:]
    width = factor_rows.shape[1]
    tokens = token_rows.shape[0] * ranks
    blocks, _, cols = grads.shape
    flops = 2 * width * rank * token_rows.shape[0]

    wide_columns = blocks * cols // YS
    chunk = wide_columns // ZS
    blocked = jax.ShapeDtypeStruct((blocks * YS, cols // YS, rows), bf)

    near = gather(basis_old[0], Y, YS)
    old_basis = lax.all_gather(near, "z", axis=0, tiled=False)
    place = lax.axis_index(Y).astype(jnp.int32).reshape(1)
    vmem, smem = pl.BlockSpec(memory_space=pltpu.VMEM), pl.BlockSpec(memory_space=pltpu.SMEM)
    side = lax.axis_index("yside").astype(jnp.int32).reshape(1)

    def swap(part):
        return lax.ppermute(part, "yside", [(0, 1), (1, 0)])

    tokens_here = token_rows.shape[0]
    got = swap(
        call(
            deal_kernel,
            jax.ShapeDtypeStruct((tokens_here, width // 2), bf),
            flops // 64,
            "deal",
            in_specs=[smem, vmem],
        )(side, token_rows)
    )
    slab = lax.cond(
        lax.axis_index("z") < ZS,
        lambda v: exchange(call(turn_kernel, blocked, flops // 64, "turn")(v), LAYER + Y),
        lambda _: jnp.zeros(blocked.shape, bf),
        grads,
    )
    old_basis, slab, got = lax.optimization_barrier((old_basis, slab, got))
    turned = call(
        project_kernel, jax.ShapeDtypeStruct((rank, tokens_here), bf), flops, "project"
    )(token_rows, old_basis)
    turned, old_basis = lax.optimization_barrier((turned, old_basis))
    moved = call(
        moved_kernel, jax.ShapeDtypeStruct((rows, rank), f4), flops // 2, "moved"
    )(factor_rows, old_basis)
    other = swap(turned)
    other, moved = lax.optimization_barrier((other, moved))
    parts = call(
        token_kernel,
        jax.ShapeDtypeStruct((ranks // 2, rank, rows), bf),
        flops,
        "tokens",
        in_specs=[smem] + [vmem] * 4,
    )(side, turned, other, token_rows, got)
    parts = exchange(parts, ("ypair", "z"))

    def applied_body(*refs):
        applied_kernel(*refs, share=(1.0 - decay_rate) / tokens, scale=math.sqrt(width))

    applied, applied_rows = call(
        applied_body,
        (
            jax.ShapeDtypeStruct((YS, rows, rank), f4),
            jax.ShapeDtypeStruct((rows, rank), f4),
        ),
        flops // 2,
        "applied",
    )(parts, moved)
    applied = exchange(applied, Y)
    cross = call(
        cross_kernel, jax.ShapeDtypeStruct((wide_columns, rank), f4), flops // 2, "cross"
    )(applied, slab)
    cross, applied = lax.optimization_barrier((cross, applied))
    cross = lax.psum_scatter(cross, "z", scatter_dimension=0, tiled=True)
    gram = call(gram_kernel, jax.ShapeDtypeStruct((rank, rank), f4), flops, "gram")(applied)
    factor_out = (
        jax.ShapeDtypeStruct((rank, rank), f4),
        jax.ShapeDtypeStruct((1, rank), bf),
        jax.ShapeDtypeStruct((1, rank), f4),
    )

    def factored(gram):
        parts = exchange(gram.reshape(ZS, rank // ZS, rank), "z")
        total = call(
            sum_kernel, jax.ShapeDtypeStruct((ZS, rank // ZS, rank), f4), flops // 64, "sum"
        )(parts)
        total = exchange(total, "z").reshape(rank, rank)
        return call(factor_kernel, factor_out, 20 * flops, "factor")(total)

    inverse, eigen, scale = lax.cond(
        lax.axis_index("z") < ZS,
        factored,
        lambda _: tuple(jnp.zeros(v.shape, v.dtype) for v in factor_out),
        gram,
    )
    wide_fresh, fresh = call(
        fresh_kernel,
        (
            jax.ShapeDtypeStruct((YS, rows, rank), bf),
            jax.ShapeDtypeStruct((rows, rank), bf),
        ),
        2 * flops,
        "fresh",
        in_specs=[smem, vmem, vmem],
    )(place, applied, inverse)
    cross, wide_fresh = lax.optimization_barrier((cross, wide_fresh))
    scaled = call(
        scale_kernel,
        jax.ShapeDtypeStruct((ZS, chunk, rank), bf),
        flops // 8,
        "scale",
    )(cross, inverse, scale)
    scaled = exchange(scaled, "z")
    result = call(result_kernel, blocked, flops // 2, "result")(wide_fresh, scaled, slab)
    result = exchange(result, LAYER + Y)
    conditioned = call(
        turn_back_kernel,
        jax.ShapeDtypeStruct((blocks, rows, cols), bf),
        flops // 64,
        "turn_back",
    )(result)
    return (fresh[None], eigen, conditioned, applied_rows[None])


def solution(mesh):
    fine = Mesh(mesh.devices.reshape(4, 2, 2, YS // 2, 2, ZS), LAYER + DP)
    in_specs = (
        P(LAYER, DP, None),
        P(LAYER, DP, None),
        P(LAYER, DP, None),
        P(None, DP, LAYER),
    )
    out_specs = (
        P(LAYER, DP, None),
        P(LAYER, None),
        P(None, DP, LAYER),
        P(LAYER, DP, None),
    )
    return jax.shard_map(
        per_device, mesh=fine, in_specs=in_specs, out_specs=out_specs, check_vma=False
    )
```

```python
import math

import jax
import jax.numpy as jnp
from jax import lax
from jax.experimental import pallas as pl
from jax.experimental.pallas import tpu as pltpu
from jax.sharding import Mesh, PartitionSpec as P

decay_rate = 0.25
damping = 2.0
f4 = jnp.float32
bf = jnp.bfloat16
PANEL = 32

LAYER = ("x", "yhi", "core")
Y = ("ypair", "yside")
DP = Y + ("z",)
YS, ZS = 4, 8

TN = (((0,), (0,)), ((), ()))
NN = (((1,), (0,)), ((), ()))
NT = (((1,), (1,)), ((), ()))


def exchange(parts, axis):
    return lax.all_to_all(parts, axis, split_axis=0, concat_axis=0, tiled=True)


def gather(part, axis, copies):
    return exchange(jnp.broadcast_to(part[None], (copies,) + part.shape), axis)


def call(body, outs, flops, name, **more):
    return pl.pallas_call(
        body,
        out_shape=outs,
        **more,
        name=name,
        cost_estimate=pl.CostEstimate(flops=flops, bytes_accessed=1 << 20, transcendentals=0),
        compiler_params=pltpu.CompilerParams(vmem_limit_bytes=24 << 20),
    )


def dot(a, b, dims):
    return lax.dot_general(a, b, dims, preferred_element_type=f4)


def split(v):
    hi = v.astype(bf)
    rest = v - hi.astype(f4)
    mid = rest.astype(bf)
    return hi, mid, (rest - mid.astype(f4)).astype(bf)


def exact_dot(a, b, dims):
    (ca,), (cb,) = dims[0]
    h, m, l = split(a)
    left = jnp.concatenate([h, h, m, m, h, l], axis=ca)
    h, m, l = split(b)
    right = jnp.concatenate([h, m, h, m, l, h], axis=cb)
    return dot(left, right, dims)


def columns(ref, pair, side, quarter, first=0, count=None):
    at = (2 * pair + side) * quarter + first
    return ref[:, pl.ds(pl.multiple_of(at, 128), count or quarter)]


def deal_kernel(place_ref, acts_ref, out_ref):
    quarter = out_ref.shape[1] // 2
    for pair in range(2):
        out_ref[:, pair * quarter : (pair + 1) * quarter] = columns(
            acts_ref, pair, 1 - place_ref[0], quarter
        )


def project_kernel(acts_ref, basis_ref, turned_ref):
    turned_ref[...] = basis_product(acts_ref, basis_ref).T.astype(bf)


def token_kernel(place_ref, turned_ref, other_ref, acts_ref, got_ref, parts_ref):
    parts, _, rows = parts_ref.shape
    zs = parts // 2
    quarter = zs * rows
    for pair in range(2):
        for z in range(0, zs, 2):
            own = columns(acts_ref, pair, place_ref[0], quarter, z * rows, 2 * rows)
            at = pair * quarter + z * rows
            both = dot(turned_ref[...], own, NN)
            both += dot(other_ref[...], got_ref[:, at : at + 2 * rows], NN)
            parts_ref[pair * zs + z] = both[:, :rows].astype(bf)
            parts_ref[pair * zs + z + 1] = both[:, rows:].astype(bf)


def basis_product(left_ref, basis_ref):
    zs, ys, rows, rank = basis_ref.shape
    total = jnp.zeros((left_ref.shape[0], rank), f4)
    for y in range(ys):
        for z in range(0, zs, 2):
            at = (y * zs + z) * rows
            block = jnp.concatenate([basis_ref[z, y], basis_ref[z + 1, y]], axis=0)
            total += dot(left_ref[:, at : at + 2 * rows], block, NN)
    return total


def moved_kernel(factor_ref, basis_ref, moved_ref):
    moved_ref[...] = decay_rate * basis_product(factor_ref, basis_ref)


def applied_kernel(parts_ref, moved_ref, applied_ref, rows_ref, *, share, scale):
    total = parts_ref[0].astype(f4)
    for j in range(1, parts_ref.shape[0]):
        total = total + parts_ref[j].astype(f4)
    applied = moved_ref[...] + share * total.T
    applied_ref[...] = jnp.broadcast_to(applied[None], applied_ref.shape)
    rows_ref[...] = applied * scale


def turn_kernel(grads_ref, turned_ref):
    blocks, quarter = grads_ref.shape[0], turned_ref.shape[1]
    share = grads_ref.shape[2] // quarter
    for b in range(blocks):
        turned = grads_ref[b].astype(f4).T.astype(bf)
        for q in range(share):
            turned_ref[b * share + q] = turned[q * quarter : (q + 1) * quarter]


def turn_back_kernel(turned_ref, out_ref):
    blocks, quarter = out_ref.shape[0], turned_ref.shape[1]
    share = out_ref.shape[2] // quarter
    for b in range(blocks):
        block = jnp.concatenate([turned_ref[b * share + q] for q in range(share)], axis=0)
        out_ref[b] = block.astype(f4).T.astype(bf)


def slab_of(slab_ref, y, ys):
    return jnp.concatenate([slab_ref[j] for j in range(y, slab_ref.shape[0], ys)], axis=0)


def cross_kernel(applied_ref, slab_ref, cross_ref):
    ys, quarter = applied_ref.shape[0], slab_ref.shape[1]
    split_rows = [split(applied_ref[y]) for y in range(ys)]
    both = jnp.concatenate([v[0] for v in split_rows] + [v[1] for v in split_rows], axis=0)
    group = 4
    for j in range(0, slab_ref.shape[0] // ys, group):
        blocks = []
        for y in range(ys):
            held = [slab_ref[i * ys + y] for i in range(j, j + group)]
            blocks.append(jnp.concatenate(held, axis=0))
        left = jnp.concatenate(blocks + blocks, axis=1)
        cross_ref[j * quarter : (j + group) * quarter] = dot(left, both, NN)


def gram_kernel(applied_ref, gram_ref):
    applied = jnp.concatenate([applied_ref[j] for j in range(applied_ref.shape[0])], axis=0)
    gram_ref[...] = exact_dot(applied, applied, TN)


def sum_kernel(parts_ref, total_ref):
    total = parts_ref[0]
    for j in range(1, parts_ref.shape[0]):
        total = total + parts_ref[j]
    total_ref[...] = jnp.broadcast_to(total[None], total_ref.shape)


def reciprocal(x):
    r = pl.reciprocal(x, approx=True)
    r = r * (2.0 - x * r)
    return r * (2.0 - x * r)


def invert_factor(ref):
    n = ref.shape[0]
    halves = n // 128
    lane = lax.broadcasted_iota(jnp.int32, (8, 128), 1)
    row = lax.broadcasted_iota(jnp.int32, (8, 128), 0)

    def read(r, count, q):
        return ref[r : r + count, q * 128 : (q + 1) * 128]

    def write(r, count, q, v):
        ref[r : r + count, q * 128 : (q + 1) * 128] = v

    def splat(v, i, j):
        return jnp.broadcast_to(v[j // 128][i : i + 1, j % 128 : j % 128 + 1], (8, 128))

    def lanes(v, j):
        return jnp.broadcast_to(v[j // 128][:, j % 128 : j % 128 + 1], (8, 128))

    def rows(v, i):
        return [jnp.broadcast_to(h[i : i + 1, :], (8, 128)) for h in v]

    steps = PANEL // 8
    for p0 in range(0, n, PANEL):
        slabs = [[read(p0 + 8 * s, 8, q) for q in range(halves)] for s in range(steps)]
        for s in range(steps):
            k0 = p0 + 8 * s
            v = slabs[s]
            d = [[splat(v, i, k0 + j) for j in range(i + 1)] for i in range(8)]
            low = [[None] * 8 for _ in range(8)]
            root = []
            for j in range(8):
                r = reciprocal(d[j][j])
                root.append(lax.rsqrt(d[j][j]))
                for i in range(j + 1, 8):
                    low[i][j] = d[i][j] * r
                for k in range(j + 1, 8):
                    for i in range(k, 8):
                        d[i][k] = d[i][k] - low[i][j] * d[k][j]
            w = [[None] * 8 for _ in range(8)]
            for j in range(8):
                for i in range(j + 1, 8):
                    t = low[i][j]
                    for m in range(j + 1, i):
                        t = t + low[i][m] * w[m][j]
                    w[i][j] = -t
            for i in range(8):
                for j in range(i):
                    w[i][j] = w[i][j] * root[i]
                w[i][i] = root[i]
            src = list(v)
            h = k0 // 128
            off = lane + (h * 128 - k0)
            inside = (off >= 0) & (off < 8)
            src[h] = jnp.where(inside, jnp.where(off == row, 1.0, 0.0), v[h])
            new = [jnp.zeros((8, 128), f4) for _ in range(halves)]
            for m in range(8):
                column = jnp.where(row >= m, w[m][m], 0.0)
                for i in range(m + 1, 8):
                    column = jnp.where(row >= i, w[i][m], column)
                source = rows(src, m)
                new = [new[q] + column * source[q] for q in range(halves)]
            slabs[s] = new
            for q in range(halves):
                write(k0, 8, q, new[q])
            spread = [rows(new, j) for j in range(8)] if s < steps - 1 else None
            for t in range(s + 1, steps):
                u = slabs[t]
                b = [lanes(u, k0 + m) for m in range(8)]
                cur = list(u)
                cur[h] = jnp.where(inside, 0.0, u[h])
                for j in range(8):
                    c = w[j][0] * b[0]
                    for m in range(1, j + 1):
                        c = c + w[j][m] * b[m]
                    cur = [cur[q] - c * spread[j][q] for q in range(halves)]
                slabs[t] = cur
        e0 = p0 + PANEL
        if e0 < n:
            top = jnp.concatenate([jnp.concatenate(v, axis=1) for v in slabs], axis=0)
            ahead = lax.broadcasted_iota(jnp.int32, (PANEL, n), 1) - p0
            below = lax.broadcasted_iota(jnp.int32, (PANEL, n), 0)
            kept = jnp.where((ahead > below) & (ahead < PANEL), 0.0, top)
            out = exact_dot(top, kept, TN)
            for q in range(halves):
                old = read(e0, n - e0, q)
                at = lax.broadcasted_iota(jnp.int32, (n - e0, 128), 1) + (q * 128 - p0)
                old = jnp.where((at >= 0) & (at < PANEL), 0.0, old)
                write(e0, n - e0, q, old - out[e0:, q * 128 : (q + 1) * 128])


def factor_kernel(gram_ref, inverse_ref, eigen_ref, scale_ref):
    n = gram_ref.shape[0]
    inverse_ref[...] = gram_ref[...]
    invert_factor(inverse_ref)
    a = lax.broadcasted_iota(jnp.int32, (n, n), 0)
    b = lax.broadcasted_iota(jnp.int32, (n, n), 1)
    inverse = jnp.where(a >= b, inverse_ref[...], 0.0)
    inverse_ref[...] = inverse
    diagonal = jnp.sum(jnp.where(a == b, inverse, 0.0), axis=0, keepdims=True)
    eigen = (1.0 / diagonal).astype(bf)
    eigen_ref[...] = eigen
    scale_ref[...] = 1.0 / (eigen.astype(f4) + damping) - 1.0 / damping


def fresh_kernel(place_ref, applied_ref, inverse_ref, fresh_ref, own_ref):
    ys, rows, _ = applied_ref.shape
    applied = jnp.concatenate([applied_ref[y] for y in range(ys)], axis=0)
    fresh = exact_dot(applied, inverse_ref[...], NT).astype(bf)
    for y in range(ys):
        fresh_ref[y] = fresh[y * rows : (y + 1) * rows]
    own_ref[...] = fresh_ref[place_ref[0]]


def scale_kernel(cross_ref, inverse_ref, scale_ref, scaled_ref):
    coupling = exact_dot(cross_ref[...], inverse_ref[...], NT)
    scaled = (coupling * scale_ref[...]).astype(bf)
    for j in range(scaled_ref.shape[0]):
        scaled_ref[j] = scaled


def result_kernel(fresh_ref, scaled_ref, slab_ref, out_ref):
    ys, quarter = fresh_ref.shape[0], slab_ref.shape[1]
    scaled = jnp.concatenate([scaled_ref[j] for j in range(scaled_ref.shape[0])], axis=0)
    for y in range(ys):
        moved = dot(scaled, fresh_ref[y], NT)
        result = (slab_of(slab_ref, y, ys).astype(f4) / damping + moved).astype(bf)
        for j in range(out_ref.shape[0] // ys):
            out_ref[j * ys + y] = result[j * quarter : (j + 1) * quarter]


def per_device(acts, factor_old, basis_old, grads):
    token_rows, factor_rows = acts[0], factor_old[0]
    ranks = YS * ZS
    rows, rank = basis_old.shape[1:]
    width = factor_rows.shape[1]
    tokens = token_rows.shape[0] * ranks
    blocks, _, cols = grads.shape
    flops = 2 * width * rank * token_rows.shape[0]

    wide_columns = blocks * cols // YS
    chunk = wide_columns // ZS
    blocked = jax.ShapeDtypeStruct((blocks * YS, cols // YS, rows), bf)

    near = gather(basis_old[0], Y, YS)
    old_basis = lax.all_gather(near, "z", axis=0, tiled=False)
    place = lax.axis_index(Y).astype(jnp.int32).reshape(1)
    vmem, smem = pl.BlockSpec(memory_space=pltpu.VMEM), pl.BlockSpec(memory_space=pltpu.SMEM)
    side = lax.axis_index("yside").astype(jnp.int32).reshape(1)

    def swap(part):
        return lax.ppermute(part, "yside", [(0, 1), (1, 0)])

    tokens_here = token_rows.shape[0]
    got = swap(
        call(
            deal_kernel,
            jax.ShapeDtypeStruct((tokens_here, width // 2), bf),
            flops // 64,
            "deal",
            in_specs=[smem, vmem],
        )(side, token_rows)
    )
    slab = lax.cond(
        lax.axis_index("z") < ZS,
        lambda v: exchange(call(turn_kernel, blocked, flops // 64, "turn")(v), LAYER + Y),
        lambda _: jnp.zeros(blocked.shape, bf),
        grads,
    )
    old_basis, slab, got = lax.optimization_barrier((old_basis, slab, got))
    turned = call(
        project_kernel, jax.ShapeDtypeStruct((rank, tokens_here), bf), flops, "project"
    )(token_rows, old_basis)
    turned, old_basis = lax.optimization_barrier((turned, old_basis))
    moved = call(
        moved_kernel, jax.ShapeDtypeStruct((rows, rank), f4), flops // 2, "moved"
    )(factor_rows, old_basis)
    other = swap(turned)
    other, moved = lax.optimization_barrier((other, moved))
    parts = call(
        token_kernel,
        jax.ShapeDtypeStruct((ranks // 2, rank, rows), bf),
        flops,
        "tokens",
        in_specs=[smem] + [vmem] * 4,
    )(side, turned, other, token_rows, got)
    parts = exchange(parts, ("ypair", "z"))

    def applied_body(*refs):
        applied_kernel(*refs, share=(1.0 - decay_rate) / tokens, scale=math.sqrt(width))

    applied, applied_rows = call(
        applied_body,
        (
            jax.ShapeDtypeStruct((YS, rows, rank), f4),
            jax.ShapeDtypeStruct((rows, rank), f4),
        ),
        flops // 2,
        "applied",
    )(parts, moved)
    applied = exchange(applied, Y)
    cross = call(
        cross_kernel, jax.ShapeDtypeStruct((wide_columns, rank), f4), flops // 2, "cross"
    )(applied, slab)
    cross, applied = lax.optimization_barrier((cross, applied))
    cross = lax.psum_scatter(cross, "z", scatter_dimension=0, tiled=True)
    gram = call(gram_kernel, jax.ShapeDtypeStruct((rank, rank), f4), flops, "gram")(applied)
    factor_out = (
        jax.ShapeDtypeStruct((rank, rank), f4),
        jax.ShapeDtypeStruct((1, rank), bf),
        jax.ShapeDtypeStruct((1, rank), f4),
    )

    def factored(gram):
        parts = exchange(gram.reshape(ZS, rank // ZS, rank), "z")
        total = call(
            sum_kernel, jax.ShapeDtypeStruct((ZS, rank // ZS, rank), f4), flops // 64, "sum"
        )(parts)
        total = exchange(total, "z").reshape(rank, rank)
        return call(factor_kernel, factor_out, 20 * flops, "factor")(total)

    inverse, eigen, scale = lax.cond(
        lax.axis_index("z") < ZS,
        factored,
        lambda _: tuple(jnp.zeros(v.shape, v.dtype) for v in factor_out),
        gram,
    )
    wide_fresh, fresh = call(
        fresh_kernel,
        (
            jax.ShapeDtypeStruct((YS, rows, rank), bf),
            jax.ShapeDtypeStruct((rows, rank), bf),
        ),
        2 * flops,
        "fresh",
        in_specs=[smem, vmem, vmem],
    )(place, applied, inverse)
    cross, wide_fresh = lax.optimization_barrier((cross, wide_fresh))
    scaled = call(
        scale_kernel,
        jax.ShapeDtypeStruct((ZS, chunk, rank), bf),
        flops // 8,
        "scale",
    )(cross, inverse, scale)
    scaled = exchange(scaled, "z")
    result = call(result_kernel, blocked, flops // 2, "result")(wide_fresh, scaled, slab)
    result = exchange(result, LAYER + Y)
    conditioned = call(
        turn_back_kernel,
        jax.ShapeDtypeStruct((blocks, rows, cols), bf),
        flops // 64,
        "turn_back",
    )(result)
    return (fresh[None], eigen, conditioned, applied_rows[None])


def solution(mesh):
    fine = Mesh(mesh.devices.reshape(4, 2, 2, YS // 2, 2, ZS), LAYER + DP)
    in_specs = (
        P(LAYER, DP, None),
        P(LAYER, DP, None),
        P(LAYER, DP, None),
        P(None, DP, LAYER),
    )
    out_specs = (
        P(LAYER, DP, None),
        P(LAYER, None),
        P(None, DP, LAYER),
        P(LAYER, DP, None),
    )
    return jax.shard_map(
        per_device, mesh=fine, in_specs=in_specs, out_specs=out_specs, check_vma=False
    )
```
